32 devices in a mesh: dp: 4 (over y, core), seq: 8 (over z, x).
Axes of the slice: x: 2, y: 2, z: 4, core: 2. Of those that a mesh axis runs over, the one named last changes fastest.
Arguments:
- tokens: bfloat16 [8, 1024, 768], P('dp', 'seq'), may hold values from -8 to 8
- segments: int32 [8, 1024], P('dp'), may hold values from 0 to 3, as said below
- cotangent: bfloat16 [8, 1024, 768], P('dp', 'seq'), may hold values from -6 to 6
- w_qkv: bfloat16 [768, 2304], P(('dp', 'seq')), may hold values from -0.21875 to 0.21875
- bias_q: bfloat16 [768], P(('dp', 'seq')), may hold values from -3 to 3
- bias_v: bfloat16 [768], P(('dp', 'seq')), may hold values from -0.3125 to 0.3125
- w_out: bfloat16 [768, 768], P(('dp', 'seq')), may hold values from -3 to 3
- bias_out: bfloat16 [768], P(('dp', 'seq')), may hold values from -3 to 3
- gain_one: bfloat16 [768], P(('dp', 'seq')), may hold values from 0.099609375 to 1.8984375
- shift_one: bfloat16 [768], P(('dp', 'seq')), may hold values from -1.75 to 1.75
- w_up: bfloat16 [768, 3072], P(('dp', 'seq')), may hold values from -0.21875 to 0.21875
- bias_up: bfloat16 [3072], P(('dp', 'seq')), may hold values from -3 to 3
- w_down: bfloat16 [3072, 768], P(('dp', 'seq')), may hold values from -0.109375 to 0.109375
- bias_down: bfloat16 [768], P(('dp', 'seq')), may hold values from -3 to 3
- gain_two: bfloat16 [768], P(('dp', 'seq')), may hold values from 0.099609375 to 1.8984375
- shift_two: bfloat16 [768], P(('dp', 'seq')), may hold values from -1.75 to 1.75
Outputs:
- layer_out: bfloat16 [8, 1024, 768], P('dp', 'seq')
- grad_tokens: float32 [8, 1024, 768], P('dp', 'seq')
- grad_w_qkv: float32 [768, 2304], P(('dp', 'seq'))
- grad_bias_q: float32 [768], P(('dp', 'seq'))
- grad_bias_v: float32 [768], P(('dp', 'seq'))
- grad_w_out: float32 [768, 768], P(('dp', 'seq'))
- grad_bias_out: float32 [768], P(('dp', 'seq'))
- grad_gain_one: float32 [768], P(('dp', 'seq'))
- grad_shift_one: float32 [768], P(('dp', 'seq'))
- grad_w_up: float32 [768, 3072], P(('dp', 'seq'))
- grad_bias_up: float32 [3072], P(('dp', 'seq'))
- grad_w_down: float32 [3072, 768], P(('dp', 'seq'))
- grad_bias_down: float32 [768], P(('dp', 'seq'))
- grad_gain_two: float32 [768], P(('dp', 'seq'))
- grad_shift_two: float32 [768], P(('dp', 'seq'))
The draws below stay inside these ranges and needn't reach their ends.
Inputs may be any that keep to these rules, and one draw needn't show every extreme that they name: `segments`: along each sequence the numbers start at 0 and never fall; a token attends to the tokens of its own sequence with its own number. In one sequence, drawn from the seed, of the 2 of each index of dp all numbers are 0.
All inputs are finite; a program needn't handle non-finite values.
Results may differ from the reference program's by a relative error of at most 0.015.
Values may be sent and summed in bfloat16 or wider, within the bound.
A program may use at most 192 MiB of HBM per device.

```python
import jax
import jax.numpy as jnp
from jax import lax

D = 768
HEADS = 12
HEAD = 64
FF = 3072
SEQ_DEV = 2
LENGTH = 1024
SEQS = 8
NCUT = 3


def draw_segments(key, part):
    key = jax.random.fold_in(key, 7)
    cut_key, pick_key = jax.random.split(key)
    cut_points = jax.random.randint(cut_key, (SEQS, NCUT), 1, LENGTH)
    groups = SEQS // SEQ_DEV
    chosen = jax.random.randint(pick_key, (groups,), 0, SEQ_DEV)
    seq_ids = jnp.arange(SEQS)
    whole_seq = seq_ids % SEQ_DEV == chosen[seq_ids // SEQ_DEV]
    cut_points = jnp.where(whole_seq[:, None], LENGTH, cut_points)
    positions = jnp.arange(LENGTH)
    passed = (cut_points[:, None, :] <= positions[None, :, None]).astype(jnp.int32)
    return jnp.sum(passed, axis=-1).astype(jnp.int32)


def strengthened(array, rng, source, target, blocks, factor):
    owner, partner = [(jnp.arange(array.shape[axis_at]) // (array.shape[axis_at] // blocks)).reshape([-1 if axis == axis_at else 1 for axis in range(array.ndim)]) for axis_at in (source, target)]
    chosen = jax.random.permutation(rng, blocks)[partner]
    strong = (owner == chosen) | (owner == (partner + blocks // 2) % blocks)
    return jnp.where(strong, factor * array, array)


def block_scale(own_key, dims, cuts, low, high):
    level, own = 1.0, jax.random.fold_in(own_key, 6)
    for axis_at, parts in cuts:
        heights = jnp.exp(jax.random.uniform(jax.random.fold_in(own, axis_at), (parts,), jnp.float32, low / len(cuts), high / len(cuts)))
        level = level * jnp.repeat(heights, dims[axis_at] // parts).reshape([-1 if axis == axis_at else 1 for axis in range(len(dims))])
    return level


def normal_values(rng, shape, width, most, cuts=(), dtype=jnp.bfloat16):
    array = width * jax.random.normal(rng, shape, jnp.float32)
    if cuts:
        array = array * block_scale(rng, shape, cuts, -0.22, 0.18)
    return jnp.clip(array, -most, most).astype(dtype)


def heavy_noise(key, shape, width, most, cuts, heavy, dtype=jnp.bfloat16):
    entries = width * jax.random.normal(key, shape, jnp.float32)
    if cuts:
        entries = entries * block_scale(key, shape, cuts, -0.22, 0.18)
    return jnp.clip(strengthened(entries, jax.random.fold_in(key, 3), *heavy), -most, most).astype(dtype)


def setup_inputs(seed: int = 0) -> dict:
    arg_keys = jax.random.split(jax.random.key(seed), 17)
    tokens = heavy_noise(arg_keys[0], (SEQS, LENGTH, D), 1.0, 8.0, ((0, 4), (1, 8)), (1, 2, 8, 2.0))
    segments = draw_segments(jax.random.fold_in(arg_keys[16], 71), 0)
    cotangent = normal_values(arg_keys[2], (SEQS, LENGTH, D), 1.0, 6.0, ((0, 4), (1, 8)))
    w_qkv = normal_values(arg_keys[3], (D, 3 * D), D ** -0.5, 0.21875, ((0, 32),))
    bias_q = normal_values(arg_keys[4], (D,), 0.5, 3.0, ((0, 32),))
    bias_v = normal_values(arg_keys[5], (D,), 0.05, 0.3125, ((0, 32),))
    w_out = normal_values(arg_keys[6], (D, D), (max(1, D // 192)) ** -0.5, 3.0, ((0, 32),))
    bias_out = normal_values(arg_keys[7], (D,), 0.5, 3.0, ((0, 32),))
    gain_one = jnp.clip(1.0 + 0.18 * jax.random.normal(arg_keys[8], (D,), jnp.float32), 0.099609375, 1.8984375).astype(jnp.bfloat16)
    shift_one = normal_values(arg_keys[9], (D,), 0.3, 1.75, ((0, 32),))
    w_up = normal_values(arg_keys[10], (D, FF), D ** -0.5, 0.21875, ((0, 32),))
    bias_up = normal_values(arg_keys[11], (FF,), 0.5, 3.0, ((0, 32),))
    w_down = normal_values(arg_keys[12], (FF, D), FF ** -0.5, 0.109375, ((0, 32),))
    bias_down = normal_values(arg_keys[13], (D,), 0.5, 3.0, ((0, 32),))
    gain_two = jnp.clip(1.0 + 0.18 * jax.random.normal(arg_keys[14], (D,), jnp.float32), 0.099609375, 1.8984375).astype(jnp.bfloat16)
    shift_two = normal_values(arg_keys[15], (D,), 0.3, 1.75, ((0, 32),))
    return dict(tokens=tokens, segments=segments, cotangent=cotangent, w_qkv=w_qkv, bias_q=bias_q, bias_v=bias_v, w_out=w_out, bias_out=bias_out, gain_one=gain_one, shift_one=shift_one, w_up=w_up, bias_up=bias_up, w_down=w_down, bias_down=bias_down, gain_two=gain_two, shift_two=shift_two)


masked_out = -1000000000.0
epsilon = 1e-05

@jax.custom_vjp
def low(v):
    return lax.optimization_barrier(v.astype(jnp.bfloat16)).astype(jnp.float32)

@jax.custom_vjp
def low_back(v):
    return v

def low_keep(v):
    return (low(v), None)

def low_pass(kept, grad):
    return (grad,)

def back_keep(v):
    return (v, None)

def back_low(kept, grad):
    return (low(grad),)
low.defvjp(low_keep, low_pass)
low_back.defvjp(back_keep, back_low)

def normalize(values, gain_row, offset):
    center = values - lax.optimization_barrier(jnp.mean(values, axis=-1, keepdims=True))
    spread = lax.optimization_barrier(jnp.mean(center * center, axis=-1, keepdims=True))
    return center * lax.rsqrt(spread + epsilon) * gain_row + offset

def matmul(first_op, second_op):
    return jnp.dot(first_op, second_op, precision=lax.Precision.HIGHEST, preferred_element_type=jnp.float32)

def one_sequence(params, inputs, documents):
    w_qkv, bias_q, bias_v, w_out, bias_out, gain_one, shift_one, w_up, bias_up, w_down, bias_down, gain_two, shift_two = params
    length = inputs.shape[0]
    qkv_bias = jnp.concatenate([bias_q, jnp.zeros((D,), jnp.float32), bias_v])
    projected = low(low_back(matmul(inputs, w_qkv) + qkv_bias))
    queries = projected[:, :D].reshape(length, HEADS, HEAD)
    keys_all = projected[:, D:2 * D].reshape(length, HEADS, HEAD)
    values_all = projected[:, 2 * D:].reshape(length, HEADS, HEAD)
    scores = jnp.einsum('qhe,khe->hqk', queries, keys_all, precision=lax.Precision.HIGHEST) * HEAD ** (-0.5)
    scores = low_back(scores)
    same_doc = documents[:, None] == documents[None, :]
    scores = jnp.where(same_doc[None], scores, masked_out)
    probs = low(jax.nn.softmax(scores, axis=-1))
    mixed = jnp.einsum('hqk,khe->qhe', probs, values_all, precision=lax.Precision.HIGHEST).reshape(length, D)
    mixed = low(low_back(mixed))
    branch = low_back(matmul(mixed, w_out) + bias_out)
    normed_one = normalize(inputs + branch, gain_one, shift_one)
    hidden = low_back(matmul(low(normed_one), w_up) + bias_up)
    activated = low(jax.nn.gelu(hidden, approximate=False))
    feed = low_back(matmul(activated, w_down) + bias_down)
    return normalize(normed_one + feed, gain_two, shift_two)

def reference(tokens, segments, cotangent, w_qkv, bias_q, bias_v, w_out, bias_out, gain_one, shift_one, w_up, bias_up, w_down, bias_down, gain_two, shift_two):
    params = tuple((argument.astype(jnp.float32) for argument in (w_qkv, bias_q, bias_v, w_out, bias_out, gain_one, shift_one, w_up, bias_up, w_down, bias_down, gain_two, shift_two)))

    def layer(weights, inputs):

        def per_seq(seq_item):
            return one_sequence(weights, seq_item[0], seq_item[1])
        return lax.map(jax.checkpoint(per_seq), (inputs, segments))
    result, pullback = jax.vjp(layer, params, tokens.astype(jnp.float32))
    grads, grad_tokens = pullback(cotangent.astype(jnp.float32))
    return (result.astype(jnp.bfloat16), grad_tokens, grads[0], grads[1], grads[2], grads[3], grads[4], grads[5], grads[6], grads[7], grads[8], grads[9], grads[10], grads[11], grads[12])
```

```python
import jax
import jax.numpy as jnp
from jax import lax
from jax.experimental import pallas as pl
from jax.experimental.pallas import tpu as pltpu
from jax.sharding import PartitionSpec as P

HEAD = 64
HEAD_GROUP = 4


masked_out = -1000000000.0
epsilon = 1e-05


def normalize(values, gain_row, offset):
    center = values - jnp.mean(values, axis=-1, keepdims=True)
    spread = jnp.mean(center * center, axis=-1, keepdims=True)
    return center * lax.rsqrt(spread + epsilon) * gain_row + offset


def exact_gelu(values):
    return jax.nn.gelu(values, approximate=False)


def contract_rows(first_op, second_op):
    return lax.dot_general(
        first_op, second_op, (((0,), (0,)), ((), ())), preferred_element_type=jnp.float32
    )


def contract_cols(first_op, second_op):
    return lax.dot_general(
        first_op, second_op, (((1,), (1,)), ((), ())), preferred_element_type=jnp.float32
    )


def column_sum(values):
    return jnp.sum(values.astype(jnp.float32), axis=0)


def group_scores(query_heads, key_heads, same_doc):
    scaled = jnp.einsum(
        "qhe,khe->hqk", query_heads, key_heads, preferred_element_type=jnp.float32
    ) * HEAD ** (-0.5)
    return jnp.where(same_doc[None], scaled, masked_out)


def head_slice(values, column, width):
    return lax.dynamic_slice_in_dim(values, column, width, 1).reshape(
        values.shape[0], HEAD_GROUP, HEAD
    )


def attend_forward(seq_item):
    queries, keys_all, values_all, same_doc = seq_item
    row_count = queries.shape[0]
    width = HEAD_GROUP * HEAD
    groups = queries.shape[1] // width

    def one_group(group_idx, state_tuple):
        outputs, log_sums = state_tuple
        column = group_idx * width
        scores = group_scores(
            head_slice(queries, column, width), head_slice(keys_all, column, width), same_doc
        )
        highest = jnp.max(scores, axis=2, keepdims=True)
        exponent = jnp.exp(scores - highest)
        denominator = jnp.sum(exponent, axis=2, keepdims=True)
        weights = (exponent / denominator).astype(jnp.bfloat16)
        combined = jnp.einsum(
            "hqk,khe->qhe",
            weights,
            head_slice(values_all, column, width),
            preferred_element_type=jnp.float32,
        )
        outputs = lax.dynamic_update_slice_in_dim(
            outputs, combined.reshape(row_count, width), column, 1
        )
        log_part = (highest + jnp.log(denominator))[:, :, 0]
        log_sums = lax.dynamic_update_slice_in_dim(log_sums, log_part, group_idx * HEAD_GROUP, 0)
        return (outputs, log_sums)

    start_state = (
        jnp.zeros((row_count, queries.shape[1]), jnp.float32),
        jnp.zeros((queries.shape[1] // HEAD, row_count), jnp.float32),
    )
    return lax.fori_loop(0, groups, one_group, start_state)


def attend_query_side(seq_item):
    queries, keys_all, values_all, same_doc, log_sums, grad_mixed = seq_item
    row_count = queries.shape[0]
    width = HEAD_GROUP * HEAD
    groups = queries.shape[1] // width
    scale_factor = HEAD ** (-0.5)

    def one_group(group_idx, state_tuple):
        grad_query, deltas = state_tuple
        column = group_idx * width
        key_heads = head_slice(keys_all, column, width)
        log_part = lax.dynamic_slice_in_dim(log_sums, group_idx * HEAD_GROUP, HEAD_GROUP, 0)
        scores = group_scores(head_slice(queries, column, width), key_heads, same_doc)
        probs = jnp.exp(scores - log_part[:, :, None])
        grad_probs = jnp.einsum(
            "qhe,khe->hqk",
            head_slice(grad_mixed, column, width),
            head_slice(values_all, column, width),
            preferred_element_type=jnp.float32,
        )
        row_delta = jnp.sum(probs * grad_probs, axis=2, keepdims=True)
        grad_scores = (probs * (grad_probs - row_delta)).astype(jnp.bfloat16)
        query_term = (
            jnp.einsum("hqk,khe->qhe", grad_scores, key_heads, preferred_element_type=jnp.float32)
            * scale_factor
        )
        grad_query = lax.dynamic_update_slice_in_dim(
            grad_query, query_term.reshape(row_count, width), column, 1
        )
        deltas = lax.dynamic_update_slice_in_dim(
            deltas, row_delta[:, :, 0], group_idx * HEAD_GROUP, 0
        )
        return (grad_query, deltas)

    start_state = (
        jnp.zeros((row_count, queries.shape[1]), jnp.float32),
        jnp.zeros((queries.shape[1] // HEAD, row_count), jnp.float32),
    )
    return lax.fori_loop(0, groups, one_group, start_state)


def attend_key_side(seq_item):
    keys_own, values_own, queries_all, grad_all, log_all, delta_all, doc_mask = seq_item
    key_count = keys_own.shape[0]
    width = HEAD_GROUP * HEAD
    groups = keys_own.shape[1] // width
    scale_factor = HEAD ** (-0.5)

    def one_group(group_idx, state_tuple):
        grad_keys, grad_values = state_tuple
        column = group_idx * width
        query_heads = head_slice(queries_all, column, width)
        grad_heads = head_slice(grad_all, column, width)
        log_part = lax.dynamic_slice_in_dim(log_all, group_idx * HEAD_GROUP, HEAD_GROUP, 0)
        delta_part = lax.dynamic_slice_in_dim(delta_all, group_idx * HEAD_GROUP, HEAD_GROUP, 0)
        scores = group_scores(query_heads, head_slice(keys_own, column, width), doc_mask)
        probs = jnp.exp(scores - log_part[:, :, None])
        probs_low = probs.astype(jnp.bfloat16)
        grad_probs = jnp.einsum(
            "qhe,khe->hqk",
            grad_heads,
            head_slice(values_own, column, width),
            preferred_element_type=jnp.float32,
        )
        grad_scores = (probs * (grad_probs - delta_part[:, :, None])).astype(jnp.bfloat16)
        key_term = (
            jnp.einsum("hqk,qhe->khe", grad_scores, query_heads, preferred_element_type=jnp.float32)
            * scale_factor
        )
        value_term = jnp.einsum(
            "hqk,qhe->khe", probs_low, grad_heads, preferred_element_type=jnp.float32
        )
        grad_keys = lax.dynamic_update_slice_in_dim(
            grad_keys, key_term.reshape(key_count, width), column, 1
        )
        grad_values = lax.dynamic_update_slice_in_dim(
            grad_values, value_term.reshape(key_count, width), column, 1
        )
        return (grad_keys, grad_values)

    model_width = keys_own.shape[1]
    start_state = (
        jnp.zeros((key_count, model_width), jnp.float32),
        jnp.zeros((key_count, model_width), jnp.float32),
    )
    return lax.fori_loop(0, groups, one_group, start_state)


def on_device_general(
    tokens,
    segments,
    cotangent,
    w_qkv,
    bias_q,
    bias_v,
    w_out,
    bias_out,
    gain_one,
    shift_one,
    w_up,
    bias_up,
    w_down,
    bias_down,
    gain_two,
    shift_two,
):
    gathered = (
        lax.all_gather(w_qkv, ("dp", "seq"), axis=0, tiled=True),
        lax.all_gather(bias_q, ("dp", "seq"), axis=0, tiled=True),
        lax.all_gather(bias_v, ("dp", "seq"), axis=0, tiled=True),
        lax.all_gather(w_out, ("dp", "seq"), axis=0, tiled=True),
        lax.all_gather(bias_out, ("dp", "seq"), axis=0, tiled=True),
        lax.all_gather(gain_one, ("dp", "seq"), axis=0, tiled=True),
        lax.all_gather(shift_one, ("dp", "seq"), axis=0, tiled=True),
        lax.all_gather(w_up, ("dp", "seq"), axis=0, tiled=True),
        lax.all_gather(bias_up, ("dp", "seq"), axis=0, tiled=True),
        lax.all_gather(w_down, ("dp", "seq"), axis=0, tiled=True),
        lax.all_gather(bias_down, ("dp", "seq"), axis=0, tiled=True),
        lax.all_gather(gain_two, ("dp", "seq"), axis=0, tiled=True),
        lax.all_gather(shift_two, ("dp", "seq"), axis=0, tiled=True),
    )
    seq_count, slice_len, model_width = tokens.shape
    row_total = seq_count * slice_len
    inputs = tokens.reshape(row_total, model_width)
    qkv_bias = jnp.concatenate(
        [
            gathered[1].astype(jnp.float32),
            jnp.zeros((model_width,), jnp.float32),
            gathered[2].astype(jnp.float32),
        ]
    )
    projected = (
        jnp.dot(inputs, gathered[0], preferred_element_type=jnp.float32) + qkv_bias
    ).astype(jnp.bfloat16)
    query_low = projected[:, :model_width].reshape(seq_count, slice_len, model_width)
    key_low = projected[:, model_width : 2 * model_width].reshape(seq_count, slice_len, model_width)
    value_low = projected[:, 2 * model_width :].reshape(seq_count, slice_len, model_width)
    keys_all, values_all = (
        lax.all_gather(key_low, "seq", axis=1, tiled=True),
        lax.all_gather(value_low, "seq", axis=1, tiled=True),
    )
    first_row = lax.axis_index("seq") * slice_len
    own_docs = lax.dynamic_slice_in_dim(segments, first_row, slice_len, 1)
    same_doc = own_docs[:, :, None] == segments[:, None, :]
    mixed, log_sums = lax.map(attend_forward, (query_low, keys_all, values_all, same_doc))
    mixed_low = mixed.reshape(row_total, model_width).astype(jnp.bfloat16)
    branch = jnp.dot(mixed_low, gathered[3], preferred_element_type=jnp.float32) + gathered[
        4
    ].astype(jnp.float32)
    normed_one, norm_one_back = jax.vjp(
        normalize,
        inputs.astype(jnp.float32) + branch,
        gathered[5].astype(jnp.float32),
        gathered[6].astype(jnp.float32),
    )
    normed_low = normed_one.astype(jnp.bfloat16)
    hidden = jnp.dot(normed_low, gathered[7], preferred_element_type=jnp.float32) + gathered[
        8
    ].astype(jnp.float32)
    activated, gelu_back = jax.vjp(exact_gelu, hidden)
    activated_low = activated.astype(jnp.bfloat16)
    feed = jnp.dot(activated_low, gathered[9], preferred_element_type=jnp.float32) + gathered[
        10
    ].astype(jnp.float32)
    result, norm_two_back = jax.vjp(
        normalize,
        normed_one + feed,
        gathered[11].astype(jnp.float32),
        gathered[12].astype(jnp.float32),
    )
    weights_back = (
        lax.all_gather(w_qkv, ("dp", "seq"), axis=0, tiled=True),
        lax.all_gather(bias_q, ("dp", "seq"), axis=0, tiled=True),
        lax.all_gather(bias_v, ("dp", "seq"), axis=0, tiled=True),
        lax.all_gather(w_out, ("dp", "seq"), axis=0, tiled=True),
        lax.all_gather(bias_out, ("dp", "seq"), axis=0, tiled=True),
        lax.all_gather(gain_one, ("dp", "seq"), axis=0, tiled=True),
        lax.all_gather(shift_one, ("dp", "seq"), axis=0, tiled=True),
        lax.all_gather(w_up, ("dp", "seq"), axis=0, tiled=True),
        lax.all_gather(bias_up, ("dp", "seq"), axis=0, tiled=True),
        lax.all_gather(w_down, ("dp", "seq"), axis=0, tiled=True),
        lax.all_gather(bias_down, ("dp", "seq"), axis=0, tiled=True),
        lax.all_gather(gain_two, ("dp", "seq"), axis=0, tiled=True),
        lax.all_gather(shift_two, ("dp", "seq"), axis=0, tiled=True),
    )
    grad_sum_two, grad_gain_two, grad_shift_two = norm_two_back(
        cotangent.reshape(row_total, model_width).astype(jnp.float32)
    )
    grad_feed = grad_sum_two.astype(jnp.bfloat16)
    grad_w_down = contract_rows(activated_low, grad_feed)
    grad_bias_down = column_sum(grad_feed)
    (grad_hidden,) = gelu_back(contract_cols(grad_feed, weights_back[9]))
    grad_hidden_low = grad_hidden.astype(jnp.bfloat16)
    grad_w_up = contract_rows(normed_low, grad_hidden_low)
    grad_bias_up = column_sum(grad_hidden_low)
    grad_normed = grad_sum_two + contract_cols(grad_hidden_low, weights_back[7])
    grad_sum_one, grad_gain_one, grad_shift_one = norm_one_back(grad_normed)
    grad_branch = grad_sum_one.astype(jnp.bfloat16)
    grad_w_out = contract_rows(mixed_low, grad_branch)
    grad_bias_out = column_sum(grad_branch)
    grad_mixed = (
        contract_cols(grad_branch, weights_back[3])
        .astype(jnp.bfloat16)
        .reshape(seq_count, slice_len, model_width)
    )
    keys_back, values_back = (
        lax.all_gather(key_low, "seq", axis=1, tiled=True),
        lax.all_gather(value_low, "seq", axis=1, tiled=True),
    )
    grad_query, row_deltas = lax.map(
        attend_query_side, (query_low, keys_back, values_back, same_doc, log_sums, grad_mixed)
    )
    queries_all, grad_mixed_all = (
        lax.all_gather(query_low, "seq", axis=1, tiled=True),
        lax.all_gather(grad_mixed, "seq", axis=1, tiled=True),
    )
    log_all, delta_all = (
        lax.all_gather(log_sums, "seq", axis=2, tiled=True),
        lax.all_gather(row_deltas, "seq", axis=2, tiled=True),
    )
    doc_mask = segments[:, :, None] == own_docs[:, None, :]
    grad_key_own, grad_value_own = lax.map(
        attend_key_side,
        (key_low, value_low, queries_all, grad_mixed_all, log_all, delta_all, doc_mask),
    )
    grad_proj = jnp.concatenate(
        [
            grad_query.astype(jnp.bfloat16),
            grad_key_own.astype(jnp.bfloat16),
            grad_value_own.astype(jnp.bfloat16),
        ],
        axis=2,
    ).reshape(row_total, 3 * model_width)
    grad_w_qkv = contract_rows(inputs, grad_proj)
    grad_bias_q = column_sum(grad_proj[:, :model_width])
    grad_bias_v = column_sum(grad_proj[:, 2 * model_width :])
    grad_inputs = grad_sum_one + contract_cols(grad_proj, weights_back[0])
    owned = (
        lax.psum_scatter(grad_w_qkv, ("dp", "seq"), scatter_dimension=0, tiled=True),
        lax.psum_scatter(grad_bias_q, ("dp", "seq"), scatter_dimension=0, tiled=True),
        lax.psum_scatter(grad_bias_v, ("dp", "seq"), scatter_dimension=0, tiled=True),
        lax.psum_scatter(grad_w_out, ("dp", "seq"), scatter_dimension=0, tiled=True),
        lax.psum_scatter(grad_bias_out, ("dp", "seq"), scatter_dimension=0, tiled=True),
        lax.psum_scatter(grad_gain_one, ("dp", "seq"), scatter_dimension=0, tiled=True),
        lax.psum_scatter(grad_shift_one, ("dp", "seq"), scatter_dimension=0, tiled=True),
        lax.psum_scatter(grad_w_up, ("dp", "seq"), scatter_dimension=0, tiled=True),
        lax.psum_scatter(grad_bias_up, ("dp", "seq"), scatter_dimension=0, tiled=True),
        lax.psum_scatter(grad_w_down, ("dp", "seq"), scatter_dimension=0, tiled=True),
        lax.psum_scatter(grad_bias_down, ("dp", "seq"), scatter_dimension=0, tiled=True),
        lax.psum_scatter(grad_gain_two, ("dp", "seq"), scatter_dimension=0, tiled=True),
        lax.psum_scatter(grad_shift_two, ("dp", "seq"), scatter_dimension=0, tiled=True),
    )
    final_out = result.astype(jnp.bfloat16).reshape(seq_count, slice_len, model_width)
    grad_tokens = grad_inputs.reshape(seq_count, slice_len, model_width)
    return (final_out, grad_tokens) + tuple(owned)


def forward_kernel(q_ref, k_ref, v_ref, row_doc, col_doc, out_ref, log_ref):
    scores = contract_cols(q_ref[0], k_ref[0]) * HEAD ** (-0.5)
    scores = jnp.where(row_doc[...] == col_doc[...], scores, masked_out)
    highest = jnp.max(scores, axis=1, keepdims=True)
    exponent = jnp.exp(scores - highest)
    denominator = jnp.sum(exponent, axis=1, keepdims=True)
    weights = (exponent * (1.0 / denominator)).astype(jnp.bfloat16)
    out_ref[0] = jnp.dot(weights, v_ref[0], preferred_element_type=jnp.float32).astype(jnp.bfloat16)
    log_ref[0] = highest + jnp.log(denominator)


def backward_kernel(q_ref, k_ref, v_ref, g_ref, log_ref, row_doc, col_doc, dq_ref, dk_ref, dv_ref):
    queries, keys, grads = q_ref[0], k_ref[0], g_ref[0]
    scores = contract_cols(queries, keys) * HEAD ** (-0.5)
    scores = jnp.where(row_doc[...] == col_doc[...], scores, masked_out)
    probs = jnp.exp(scores - log_ref[0])
    grad_probs = contract_cols(grads, v_ref[0])
    row_delta = jnp.sum(probs * grad_probs, axis=1, keepdims=True)
    grad_scores = (probs * (grad_probs - row_delta)).astype(jnp.bfloat16)
    dq_ref[0] = jnp.dot(grad_scores, keys, preferred_element_type=jnp.float32) * HEAD ** (-0.5)
    key_term = contract_rows(grad_scores, queries) * HEAD ** (-0.5)
    value_term = contract_rows(probs.astype(jnp.bfloat16), grads)

    @pl.when(pl.program_id(1) == 0)
    def _():
        dk_ref[0] = key_term
        dv_ref[0] = value_term

    @pl.when(pl.program_id(1) != 0)
    def _():
        dk_ref[0] += key_term
        dv_ref[0] += value_term


def attention_specs(heads, length, rows):
    own = pl.BlockSpec((1, rows, HEAD), lambda h, r: (h, r, 0))
    full = pl.BlockSpec((1, length, HEAD), lambda h, r: (h, 0, 0))
    column = pl.BlockSpec((1, rows, 1), lambda h, r: (h, r, 0))
    row_doc = pl.BlockSpec((rows, 1), lambda h, r: (r, 0))
    col_doc = pl.BlockSpec((1, length), lambda h, r: (0, 0))
    return own, full, column, row_doc, col_doc


def local_forward(queries, keys, values, docs):
    heads, length, _ = queries.shape
    rows = min(256, length)
    own, full, column, row_doc, col_doc = attention_specs(heads, length, rows)
    return pl.pallas_call(
        forward_kernel,
        grid=(heads, length // rows),
        in_specs=[own, full, full, row_doc, col_doc],
        out_specs=[own, column],
        out_shape=[
            jax.ShapeDtypeStruct((heads, length, HEAD), jnp.bfloat16),
            jax.ShapeDtypeStruct((heads, length, 1), jnp.float32),
        ],
        compiler_params=pltpu.CompilerParams(vmem_limit_bytes=40 * 1024 * 1024),
        cost_estimate=pl.CostEstimate(
            flops=16 * heads * length * length * HEAD,
            bytes_accessed=8 * heads * length * HEAD,
            transcendentals=heads * length * length,
        ),
    )(queries, keys, values, docs[:, None], docs[None, :])


def local_backward(queries, keys, values, grads, log_sums, docs):
    heads, length, _ = queries.shape
    rows = min(256, length)
    own, full, column, row_doc, col_doc = attention_specs(heads, length, rows)
    shape = jax.ShapeDtypeStruct((heads, length, HEAD), jnp.float32)
    return pl.pallas_call(
        backward_kernel,
        grid=(heads, length // rows),
        in_specs=[own, full, full, own, column, row_doc, col_doc],
        out_specs=[own, full, full],
        out_shape=[shape] * 3,
        compiler_params=pltpu.CompilerParams(vmem_limit_bytes=40 * 1024 * 1024),
        cost_estimate=pl.CostEstimate(
            flops=40 * heads * length * length * HEAD,
            bytes_accessed=20 * heads * length * HEAD,
            transcendentals=heads * length * length,
        ),
    )(queries, keys, values, grads, log_sums, docs[:, None], docs[None, :])


def on_device_packed(
    devices,
    ring,
    tokens,
    segments,
    cotangent,
    w_qkv,
    bias_q,
    bias_v,
    w_out,
    bias_out,
    gain_one,
    shift_one,
    w_up,
    bias_up,
    w_down,
    bias_down,
    gain_two,
    shift_two,
):
    both = ("dp", "seq")
    seq_count, slice_len, model_width = tokens.shape
    row_total = seq_count * slice_len
    own_rows = w_qkv.shape[0]
    fold = w_up.shape[1] // model_width
    down_rows = w_down.shape[0]
    vectors = (bias_q, bias_v, bias_out, gain_one, shift_one, bias_down, gain_two, shift_two)
    count = len(vectors)
    qkv_width = 3 * model_width

    rest = jnp.concatenate(
        [w_down, w_out] + [w_up[:, i * model_width : (i + 1) * model_width] for i in range(fold)],
        axis=0,
    )
    rest_all = lax.all_gather(rest, both, axis=0, tiled=False)
    extra = jnp.concatenate(
        [jnp.stack(vectors, axis=1), bias_up.reshape(own_rows, fold)], axis=1
    )
    first = jnp.concatenate(
        [w_qkv, jnp.pad(extra, ((0, 0), (0, 128 - count - fold)))], axis=1
    )
    first_all = lax.all_to_all(
        jnp.broadcast_to(first[None], (devices,) + first.shape), both, 0, 0, tiled=True
    ).reshape(devices * own_rows, qkv_width + 128)
    w_qkv_all = first_all[:, :qkv_width]
    small = first_all[:, qkv_width : qkv_width + count + fold].astype(jnp.float32)
    bq, bv, bo, g1, s1, bd, g2, s2 = [small[:, i] for i in range(count)]
    bu = small[:, count:].reshape(-1)

    inputs = tokens.reshape(row_total, model_width)
    qkv_bias = jnp.concatenate([bq, jnp.zeros((model_width,), jnp.float32), bv])
    projected = (
        jnp.dot(inputs, w_qkv_all, preferred_element_type=jnp.float32) + qkv_bias
    ).astype(jnp.bfloat16)

    groups = ring // seq_count
    width = model_width // groups
    heads = width // HEAD
    length = ring * slice_len
    sent = projected.reshape(seq_count, slice_len, 3, groups, width)
    sent = sent.transpose(0, 3, 1, 2, 4).reshape(ring, slice_len, 3 * width)
    own = lax.all_to_all(sent, "seq", 0, 0, tiled=True).reshape(length, 3, heads, HEAD)
    own = own.transpose(1, 2, 0, 3)
    own_seq = lax.axis_index("seq") // groups
    docs = lax.dynamic_index_in_dim(segments, own_seq, 0, keepdims=False)
    mixed_own, log_sums = local_forward(own[0], own[1], own[2], docs)
    mixed_sent = mixed_own.transpose(1, 0, 2).reshape(ring, slice_len, width)
    mixed = lax.all_to_all(mixed_sent, "seq", 0, 0, tiled=True)
    mixed_low = (
        mixed.reshape(seq_count, groups, slice_len, width)
        .transpose(0, 2, 1, 3)
        .reshape(row_total, model_width)
    )

    w_down_all = rest_all[:, :down_rows].reshape(-1, model_width)
    w_out_all = rest_all[:, down_rows : down_rows + own_rows].reshape(-1, model_width)
    up_start = down_rows + own_rows
    w_up_all = jnp.concatenate(
        [
            rest_all[:, up_start + i * own_rows : up_start + (i + 1) * own_rows].reshape(
                -1, model_width
            )
            for i in range(fold)
        ],
        axis=1,
    )
    branch = jnp.dot(mixed_low, w_out_all, preferred_element_type=jnp.float32) + bo
    normed_one, norm_one_back = jax.vjp(normalize, inputs.astype(jnp.float32) + branch, g1, s1)
    normed_low = normed_one.astype(jnp.bfloat16)
    hidden = jnp.dot(normed_low, w_up_all, preferred_element_type=jnp.float32) + bu
    activated, gelu_back = jax.vjp(exact_gelu, hidden)
    activated_low = activated.astype(jnp.bfloat16)
    feed = jnp.dot(activated_low, w_down_all, preferred_element_type=jnp.float32) + bd
    result, norm_two_back = jax.vjp(normalize, normed_one + feed, g2, s2)

    grad_sum_two, grad_gain_two, grad_shift_two = norm_two_back(
        cotangent.reshape(row_total, model_width).astype(jnp.float32)
    )
    grad_feed = grad_sum_two.astype(jnp.bfloat16)
    grad_w_down = contract_rows(activated_low, grad_feed).astype(jnp.bfloat16)
    grad_bias_down = column_sum(grad_feed)
    (grad_hidden,) = gelu_back(contract_cols(grad_feed, w_down_all))
    grad_hidden_low = grad_hidden.astype(jnp.bfloat16)
    grad_w_up = contract_rows(normed_low, grad_hidden_low).astype(jnp.bfloat16)
    grad_bias_up = column_sum(grad_hidden_low)
    grad_normed = grad_sum_two + contract_cols(grad_hidden_low, w_up_all)
    grad_sum_one, grad_gain_one, grad_shift_one = norm_one_back(grad_normed)
    grad_branch = grad_sum_one.astype(jnp.bfloat16)
    grad_w_out = contract_rows(mixed_low, grad_branch).astype(jnp.bfloat16)
    grad_bias_out = column_sum(grad_branch)

    packed = jnp.concatenate(
        [
            grad_w_down.reshape(devices, down_rows, model_width),
            grad_w_out.reshape(devices, own_rows, model_width),
        ]
        + [
            grad_w_up[:, i * model_width : (i + 1) * model_width].reshape(
                devices, own_rows, model_width
            )
            for i in range(fold)
        ],
        axis=1,
    )
    rest_sum = lax.psum_scatter(
        packed.reshape(-1, model_width), both, scatter_dimension=0, tiled=True
    ).astype(jnp.float32)

    grad_mixed = contract_cols(grad_branch, w_out_all).astype(jnp.bfloat16)
    grad_sent = (
        grad_mixed.reshape(seq_count, slice_len, groups, width)
        .transpose(0, 2, 1, 3)
        .reshape(ring, slice_len, width)
    )
    grad_own = lax.all_to_all(grad_sent, "seq", 0, 0, tiled=True)
    grad_own = grad_own.reshape(length, heads, HEAD).transpose(1, 0, 2)
    parts = local_backward(own[0], own[1], own[2], grad_own, log_sums, docs)
    back = jnp.stack(parts).astype(jnp.bfloat16)
    back = back.transpose(2, 0, 1, 3).reshape(ring, slice_len, 3 * width)
    back = lax.all_to_all(back, "seq", 0, 0, tiled=True)
    grad_proj = (
        back.reshape(seq_count, groups, slice_len, 3, width)
        .transpose(0, 2, 3, 1, 4)
        .reshape(row_total, qkv_width)
    )
    grad_w_qkv = contract_rows(inputs, grad_proj)
    grad_bias_q = column_sum(grad_proj[:, :model_width])
    grad_bias_v = column_sum(grad_proj[:, 2 * model_width :])
    grad_inputs = grad_sum_one + contract_cols(grad_proj, w_qkv_all)

    grads = (
        grad_bias_q,
        grad_bias_v,
        grad_bias_out,
        grad_gain_one,
        grad_shift_one,
        grad_bias_down,
        grad_gain_two,
        grad_shift_two,
    )
    extra = jnp.concatenate(
        [jnp.stack(grads, axis=1), grad_bias_up.reshape(-1, fold)], axis=1
    )
    last = jnp.concatenate(
        [grad_w_qkv, jnp.pad(extra, ((0, 0), (0, 128 - count - fold)))], axis=1
    ).astype(jnp.bfloat16)
    last = lax.all_to_all(
        last.reshape(devices, own_rows, qkv_width + 128), both, 0, 0, tiled=True
    )
    last = jnp.sum(last.astype(jnp.float32), axis=0)
    sums = [last[:, qkv_width + i] for i in range(count)]
    own_up = jnp.concatenate(
        [rest_sum[up_start + i * own_rows : up_start + (i + 1) * own_rows] for i in range(fold)],
        axis=1,
    )
    return (
        result.astype(jnp.bfloat16).reshape(seq_count, slice_len, model_width),
        grad_inputs.reshape(seq_count, slice_len, model_width),
        last[:, :qkv_width],
        sums[0],
        sums[1],
        rest_sum[down_rows : down_rows + own_rows],
        sums[2],
        sums[3],
        sums[4],
        own_up,
        last[:, qkv_width + count : qkv_width + count + fold].reshape(-1),
        rest_sum[:down_rows],
        sums[5],
        sums[6],
        sums[7],
    )


def solution(mesh):
    ring = mesh.shape["seq"]
    devices = ring * mesh.shape["dp"]

    def on_device(*arguments):
        seq_count, _, model_width = arguments[0].shape
        heads = model_width // HEAD
        if ring % seq_count == 0 and heads % (ring // seq_count) == 0:
            return on_device_packed(devices, ring, *arguments)
        return on_device_general(*arguments)

    return jax.shard_map(
        on_device,
        mesh=mesh,
        in_specs=(
            P("dp", "seq", None),
            P("dp", None),
            P("dp", "seq", None),
            P(("dp", "seq"), None),
            P(("dp", "seq")),
            P(("dp", "seq")),
            P(("dp", "seq"), None),
            P(("dp", "seq")),
            P(("dp", "seq")),
            P(("dp", "seq")),
            P(("dp", "seq"), None),
            P(("dp", "seq")),
            P(("dp", "seq"), None),
            P(("dp", "seq")),
            P(("dp", "seq")),
            P(("dp", "seq")),
        ),
        out_specs=(
            P("dp", "seq", None),
            P("dp", "seq", None),
            P(("dp", "seq"), None),
            P(("dp", "seq")),
            P(("dp", "seq")),
            P(("dp", "seq"), None),
            P(("dp", "seq")),
            P(("dp", "seq")),
            P(("dp", "seq")),
            P(("dp", "seq"), None),
            P(("dp", "seq")),
            P(("dp", "seq"), None),
            P(("dp", "seq")),
            P(("dp", "seq")),
            P(("dp", "seq")),
        ),
        check_vma=False,
    )
```

```python
import jax
import jax.numpy as jnp
from jax import lax
from jax.experimental import pallas as pl
from jax.experimental.pallas import tpu as pltpu
from jax.sharding import PartitionSpec as P

HEAD = 64
HEAD_GROUP = 4


masked_out = -1000000000.0
epsilon = 1e-05


def normalize(values, gain_row, offset):
    center = values - jnp.mean(values, axis=-1, keepdims=True)
    spread = jnp.mean(center * center, axis=-1, keepdims=True)
    return center * lax.rsqrt(spread + epsilon) * gain_row + offset


def exact_gelu(values):
    return jax.nn.gelu(values, approximate=False)


def contract_rows(first_op, second_op):
    return lax.dot_general(
        first_op, second_op, (((0,), (0,)), ((), ())), preferred_element_type=jnp.float32
    )


def contract_cols(first_op, second_op):
    return lax.dot_general(
        first_op, second_op, (((1,), (1,)), ((), ())), preferred_element_type=jnp.float32
    )


def column_sum(values):
    return jnp.sum(values.astype(jnp.float32), axis=0)


def group_scores(query_heads, key_heads, same_doc):
    scaled = jnp.einsum(
        "qhe,khe->hqk", query_heads, key_heads, preferred_element_type=jnp.float32
    ) * HEAD ** (-0.5)
    return jnp.where(same_doc[None], scaled, masked_out)


def head_slice(values, column, width):
    return lax.dynamic_slice_in_dim(values, column, width, 1).reshape(
        values.shape[0], HEAD_GROUP, HEAD
    )


def attend_forward(seq_item):
    queries, keys_all, values_all, same_doc = seq_item
    row_count = queries.shape[0]
    width = HEAD_GROUP * HEAD
    groups = queries.shape[1] // width

    def one_group(group_idx, state_tuple):
        outputs, log_sums = state_tuple
        column = group_idx * width
        scores = group_scores(
            head_slice(queries, column, width), head_slice(keys_all, column, width), same_doc
        )
        highest = jnp.max(scores, axis=2, keepdims=True)
        exponent = jnp.exp(scores - highest)
        denominator = jnp.sum(exponent, axis=2, keepdims=True)
        weights = (exponent / denominator).astype(jnp.bfloat16)
        combined = jnp.einsum(
            "hqk,khe->qhe",
            weights,
            head_slice(values_all, column, width),
            preferred_element_type=jnp.float32,
        )
        outputs = lax.dynamic_update_slice_in_dim(
            outputs, combined.reshape(row_count, width), column, 1
        )
        log_part = (highest + jnp.log(denominator))[:, :, 0]
        log_sums = lax.dynamic_update_slice_in_dim(log_sums, log_part, group_idx * HEAD_GROUP, 0)
        return (outputs, log_sums)

    start_state = (
        jnp.zeros((row_count, queries.shape[1]), jnp.float32),
        jnp.zeros((queries.shape[1] // HEAD, row_count), jnp.float32),
    )
    return lax.fori_loop(0, groups, one_group, start_state)


def attend_query_side(seq_item):
    queries, keys_all, values_all, same_doc, log_sums, grad_mixed = seq_item
    row_count = queries.shape[0]
    width = HEAD_GROUP * HEAD
    groups = queries.shape[1] // width
    scale_factor = HEAD ** (-0.5)

    def one_group(group_idx, state_tuple):
        grad_query, deltas = state_tuple
        column = group_idx * width
        key_heads = head_slice(keys_all, column, width)
        log_part = lax.dynamic_slice_in_dim(log_sums, group_idx * HEAD_GROUP, HEAD_GROUP, 0)
        scores = group_scores(head_slice(queries, column, width), key_heads, same_doc)
        probs = jnp.exp(scores - log_part[:, :, None])
        grad_probs = jnp.einsum(
            "qhe,khe->hqk",
            head_slice(grad_mixed, column, width),
            head_slice(values_all, column, width),
            preferred_element_type=jnp.float32,
        )
        row_delta = jnp.sum(probs * grad_probs, axis=2, keepdims=True)
        grad_scores = (probs * (grad_probs - row_delta)).astype(jnp.bfloat16)
        query_term = (
            jnp.einsum("hqk,khe->qhe", grad_scores, key_heads, preferred_element_type=jnp.float32)
            * scale_factor
        )
        grad_query = lax.dynamic_update_slice_in_dim(
            grad_query, query_term.reshape(row_count, width), column, 1
        )
        deltas = lax.dynamic_update_slice_in_dim(
            deltas, row_delta[:, :, 0], group_idx * HEAD_GROUP, 0
        )
        return (grad_query, deltas)

    start_state = (
        jnp.zeros((row_count, queries.shape[1]), jnp.float32),
        jnp.zeros((queries.shape[1] // HEAD, row_count), jnp.float32),
    )
    return lax.fori_loop(0, groups, one_group, start_state)


def attend_key_side(seq_item):
    keys_own, values_own, queries_all, grad_all, log_all, delta_all, doc_mask = seq_item
    key_count = keys_own.shape[0]
    width = HEAD_GROUP * HEAD
    groups = keys_own.shape[1] // width
    scale_factor = HEAD ** (-0.5)

    def one_group(group_idx, state_tuple):
        grad_keys, grad_values = state_tuple
        column = group_idx * width
        query_heads = head_slice(queries_all, column, width)
        grad_heads = head_slice(grad_all, column, width)
        log_part = lax.dynamic_slice_in_dim(log_all, group_idx * HEAD_GROUP, HEAD_GROUP, 0)
        delta_part = lax.dynamic_slice_in_dim(delta_all, group_idx * HEAD_GROUP, HEAD_GROUP, 0)
        scores = group_scores(query_heads, head_slice(keys_own, column, width), doc_mask)
        probs = jnp.exp(scores - log_part[:, :, None])
        probs_low = probs.astype(jnp.bfloat16)
        grad_probs = jnp.einsum(
            "qhe,khe->hqk",
            grad_heads,
            head_slice(values_own, column, width),
            preferred_element_type=jnp.float32,
        )
        grad_scores = (probs * (grad_probs - delta_part[:, :, None])).astype(jnp.bfloat16)
        key_term = (
            jnp.einsum("hqk,qhe->khe", grad_scores, query_heads, preferred_element_type=jnp.float32)
            * scale_factor
        )
        value_term = jnp.einsum(
            "hqk,qhe->khe", probs_low, grad_heads, preferred_element_type=jnp.float32
        )
        grad_keys = lax.dynamic_update_slice_in_dim(
            grad_keys, key_term.reshape(key_count, width), column, 1
        )
        grad_values = lax.dynamic_update_slice_in_dim(
            grad_values, value_term.reshape(key_count, width), column, 1
        )
        return (grad_keys, grad_values)

    model_width = keys_own.shape[1]
    start_state = (
        jnp.zeros((key_count, model_width), jnp.float32),
        jnp.zeros((key_count, model_width), jnp.float32),
    )
    return lax.fori_loop(0, groups, one_group, start_state)


def on_device_general(
    tokens,
    segments,
    cotangent,
    w_qkv,
    bias_q,
    bias_v,
    w_out,
    bias_out,
    gain_one,
    shift_one,
    w_up,
    bias_up,
    w_down,
    bias_down,
    gain_two,
    shift_two,
):
    gathered = (
        lax.all_gather(w_qkv, ("dp", "seq"), axis=0, tiled=True),
        lax.all_gather(bias_q, ("dp", "seq"), axis=0, tiled=True),
        lax.all_gather(bias_v, ("dp", "seq"), axis=0, tiled=True),
        lax.all_gather(w_out, ("dp", "seq"), axis=0, tiled=True),
        lax.all_gather(bias_out, ("dp", "seq"), axis=0, tiled=True),
        lax.all_gather(gain_one, ("dp", "seq"), axis=0, tiled=True),
        lax.all_gather(shift_one, ("dp", "seq"), axis=0, tiled=True),
        lax.all_gather(w_up, ("dp", "seq"), axis=0, tiled=True),
        lax.all_gather(bias_up, ("dp", "seq"), axis=0, tiled=True),
        lax.all_gather(w_down, ("dp", "seq"), axis=0, tiled=True),
        lax.all_gather(bias_down, ("dp", "seq"), axis=0, tiled=True),
        lax.all_gather(gain_two, ("dp", "seq"), axis=0, tiled=True),
        lax.all_gather(shift_two, ("dp", "seq"), axis=0, tiled=True),
    )
    seq_count, slice_len, model_width = tokens.shape
    row_total = seq_count * slice_len
    inputs = tokens.reshape(row_total, model_width)
    qkv_bias = jnp.concatenate(
        [
            gathered[1].astype(jnp.float32),
            jnp.zeros((model_width,), jnp.float32),
            gathered[2].astype(jnp.float32),
        ]
    )
    projected = (
        jnp.dot(inputs, gathered[0], preferred_element_type=jnp.float32) + qkv_bias
    ).astype(jnp.bfloat16)
    query_low = projected[:, :model_width].reshape(seq_count, slice_len, model_width)
    key_low = projected[:, model_width : 2 * model_width].reshape(seq_count, slice_len, model_width)
    value_low = projected[:, 2 * model_width :].reshape(seq_count, slice_len, model_width)
    keys_all, values_all = (
        lax.all_gather(key_low, "seq", axis=1, tiled=True),
        lax.all_gather(value_low, "seq", axis=1, tiled=True),
    )
    first_row = lax.axis_index("seq") * slice_len
    own_docs = lax.dynamic_slice_in_dim(segments, first_row, slice_len, 1)
    same_doc = own_docs[:, :, None] == segments[:, None, :]
    mixed, log_sums = lax.map(attend_forward, (query_low, keys_all, values_all, same_doc))
    mixed_low = mixed.reshape(row_total, model_width).astype(jnp.bfloat16)
    branch = jnp.dot(mixed_low, gathered[3], preferred_element_type=jnp.float32) + gathered[
        4
    ].astype(jnp.float32)
    normed_one, norm_one_back = jax.vjp(
        normalize,
        inputs.astype(jnp.float32) + branch,
        gathered[5].astype(jnp.float32),
        gathered[6].astype(jnp.float32),
    )
    normed_low = normed_one.astype(jnp.bfloat16)
    hidden = jnp.dot(normed_low, gathered[7], preferred_element_type=jnp.float32) + gathered[
        8
    ].astype(jnp.float32)
    activated, gelu_back = jax.vjp(exact_gelu, hidden)
    activated_low = activated.astype(jnp.bfloat16)
    feed = jnp.dot(activated_low, gathered[9], preferred_element_type=jnp.float32) + gathered[
        10
    ].astype(jnp.float32)
    result, norm_two_back = jax.vjp(
        normalize,
        normed_one + feed,
        gathered[11].astype(jnp.float32),
        gathered[12].astype(jnp.float32),
    )
    weights_back = (
        lax.all_gather(w_qkv, ("dp", "seq"), axis=0, tiled=True),
        lax.all_gather(bias_q, ("dp", "seq"), axis=0, tiled=True),
        lax.all_gather(bias_v, ("dp", "seq"), axis=0, tiled=True),
        lax.all_gather(w_out, ("dp", "seq"), axis=0, tiled=True),
        lax.all_gather(bias_out, ("dp", "seq"), axis=0, tiled=True),
        lax.all_gather(gain_one, ("dp", "seq"), axis=0, tiled=True),
        lax.all_gather(shift_one, ("dp", "seq"), axis=0, tiled=True),
        lax.all_gather(w_up, ("dp", "seq"), axis=0, tiled=True),
        lax.all_gather(bias_up, ("dp", "seq"), axis=0, tiled=True),
        lax.all_gather(w_down, ("dp", "seq"), axis=0, tiled=True),
        lax.all_gather(bias_down, ("dp", "seq"), axis=0, tiled=True),
        lax.all_gather(gain_two, ("dp", "seq"), axis=0, tiled=True),
        lax.all_gather(shift_two, ("dp", "seq"), axis=0, tiled=True),
    )
    grad_sum_two, grad_gain_two, grad_shift_two = norm_two_back(
        cotangent.reshape(row_total, model_width).astype(jnp.float32)
    )
    grad_feed = grad_sum_two.astype(jnp.bfloat16)
    grad_w_down = contract_rows(activated_low, grad_feed)
    grad_bias_down = column_sum(grad_feed)
    (grad_hidden,) = gelu_back(contract_cols(grad_feed, weights_back[9]))
    grad_hidden_low = grad_hidden.astype(jnp.bfloat16)
    grad_w_up = contract_rows(normed_low, grad_hidden_low)
    grad_bias_up = column_sum(grad_hidden_low)
    grad_normed = grad_sum_two + contract_cols(grad_hidden_low, weights_back[7])
    grad_sum_one, grad_gain_one, grad_shift_one = norm_one_back(grad_normed)
    grad_branch = grad_sum_one.astype(jnp.bfloat16)
    grad_w_out = contract_rows(mixed_low, grad_branch)
    grad_bias_out = column_sum(grad_branch)
    grad_mixed = (
        contract_cols(grad_branch, weights_back[3])
        .astype(jnp.bfloat16)
        .reshape(seq_count, slice_len, model_width)
    )
    keys_back, values_back = (
        lax.all_gather(key_low, "seq", axis=1, tiled=True),
        lax.all_gather(value_low, "seq", axis=1, tiled=True),
    )
    grad_query, row_deltas = lax.map(
        attend_query_side, (query_low, keys_back, values_back, same_doc, log_sums, grad_mixed)
    )
    queries_all, grad_mixed_all = (
        lax.all_gather(query_low, "seq", axis=1, tiled=True),
        lax.all_gather(grad_mixed, "seq", axis=1, tiled=True),
    )
    log_all, delta_all = (
        lax.all_gather(log_sums, "seq", axis=2, tiled=True),
        lax.all_gather(row_deltas, "seq", axis=2, tiled=True),
    )
    doc_mask = segments[:, :, None] == own_docs[:, None, :]
    grad_key_own, grad_value_own = lax.map(
        attend_key_side,
        (key_low, value_low, queries_all, grad_mixed_all, log_all, delta_all, doc_mask),
    )
    grad_proj = jnp.concatenate(
        [
            grad_query.astype(jnp.bfloat16),
            grad_key_own.astype(jnp.bfloat16),
            grad_value_own.astype(jnp.bfloat16),
        ],
        axis=2,
    ).reshape(row_total, 3 * model_width)
    grad_w_qkv = contract_rows(inputs, grad_proj)
    grad_bias_q = column_sum(grad_proj[:, :model_width])
    grad_bias_v = column_sum(grad_proj[:, 2 * model_width :])
    grad_inputs = grad_sum_one + contract_cols(grad_proj, weights_back[0])
    owned = (
        lax.psum_scatter(grad_w_qkv, ("dp", "seq"), scatter_dimension=0, tiled=True),
        lax.psum_scatter(grad_bias_q, ("dp", "seq"), scatter_dimension=0, tiled=True),
        lax.psum_scatter(grad_bias_v, ("dp", "seq"), scatter_dimension=0, tiled=True),
        lax.psum_scatter(grad_w_out, ("dp", "seq"), scatter_dimension=0, tiled=True),
        lax.psum_scatter(grad_bias_out, ("dp", "seq"), scatter_dimension=0, tiled=True),
        lax.psum_scatter(grad_gain_one, ("dp", "seq"), scatter_dimension=0, tiled=True),
        lax.psum_scatter(grad_shift_one, ("dp", "seq"), scatter_dimension=0, tiled=True),
        lax.psum_scatter(grad_w_up, ("dp", "seq"), scatter_dimension=0, tiled=True),
        lax.psum_scatter(grad_bias_up, ("dp", "seq"), scatter_dimension=0, tiled=True),
        lax.psum_scatter(grad_w_down, ("dp", "seq"), scatter_dimension=0, tiled=True),
        lax.psum_scatter(grad_bias_down, ("dp", "seq"), scatter_dimension=0, tiled=True),
        lax.psum_scatter(grad_gain_two, ("dp", "seq"), scatter_dimension=0, tiled=True),
        lax.psum_scatter(grad_shift_two, ("dp", "seq"), scatter_dimension=0, tiled=True),
    )
    final_out = result.astype(jnp.bfloat16).reshape(seq_count, slice_len, model_width)
    grad_tokens = grad_inputs.reshape(seq_count, slice_len, model_width)
    return (final_out, grad_tokens) + tuple(owned)


def forward_kernel(q_ref, k_ref, v_ref, row_doc, col_doc, out_ref, log_ref):
    scores = contract_cols(q_ref[0], k_ref[0]) * HEAD ** (-0.5)
    scores = jnp.where(row_doc[...] == col_doc[...], scores, masked_out)
    highest = jnp.max(scores, axis=1, keepdims=True)
    exponent = jnp.exp(scores - highest)
    denominator = jnp.sum(exponent, axis=1, keepdims=True)
    weights = (exponent * (1.0 / denominator)).astype(jnp.bfloat16)
    out_ref[0] = jnp.dot(weights, v_ref[0], preferred_element_type=jnp.float32).astype(jnp.bfloat16)
    log_ref[0] = highest + jnp.log(denominator)


def backward_kernel(q_ref, k_ref, v_ref, g_ref, log_ref, row_doc, col_doc, dq_ref, dk_ref, dv_ref):
    queries, keys, grads = q_ref[0], k_ref[0], g_ref[0]
    scores = contract_cols(queries, keys) * HEAD ** (-0.5)
    scores = jnp.where(row_doc[...] == col_doc[...], scores, masked_out)
    probs = jnp.exp(scores - log_ref[0])
    grad_probs = contract_cols(grads, v_ref[0])
    row_delta = jnp.sum(probs * grad_probs, axis=1, keepdims=True)
    grad_scores = (probs * (grad_probs - row_delta)).astype(jnp.bfloat16)
    dq_ref[0] = jnp.dot(grad_scores, keys, preferred_element_type=jnp.float32) * HEAD ** (-0.5)
    key_term = contract_rows(grad_scores, queries) * HEAD ** (-0.5)
    value_term = contract_rows(probs.astype(jnp.bfloat16), grads)

    @pl.when(pl.program_id(1) == 0)
    def _():
        dk_ref[0] = key_term
        dv_ref[0] = value_term

    @pl.when(pl.program_id(1) != 0)
    def _():
        dk_ref[0] += key_term
        dv_ref[0] += value_term


def attention_specs(heads, length, rows):
    own = pl.BlockSpec((1, rows, HEAD), lambda h, r: (h, r, 0))
    full = pl.BlockSpec((1, length, HEAD), lambda h, r: (h, 0, 0))
    column = pl.BlockSpec((1, rows, 1), lambda h, r: (h, r, 0))
    row_doc = pl.BlockSpec((rows, 1), lambda h, r: (r, 0))
    col_doc = pl.BlockSpec((1, length), lambda h, r: (0, 0))
    return own, full, column, row_doc, col_doc


def local_forward(queries, keys, values, docs):
    heads, length, _ = queries.shape
    rows = min(256, length)
    own, full, column, row_doc, col_doc = attention_specs(heads, length, rows)
    return pl.pallas_call(
        forward_kernel,
        grid=(heads, length // rows),
        in_specs=[own, full, full, row_doc, col_doc],
        out_specs=[own, column],
        out_shape=[
            jax.ShapeDtypeStruct((heads, length, HEAD), jnp.bfloat16),
            jax.ShapeDtypeStruct((heads, length, 1), jnp.float32),
        ],
        compiler_params=pltpu.CompilerParams(vmem_limit_bytes=40 * 1024 * 1024),
        cost_estimate=pl.CostEstimate(
            flops=16 * heads * length * length * HEAD,
            bytes_accessed=8 * heads * length * HEAD,
            transcendentals=heads * length * length,
        ),
    )(queries, keys, values, docs[:, None], docs[None, :])


def local_backward(queries, keys, values, grads, log_sums, docs):
    heads, length, _ = queries.shape
    rows = min(256, length)
    own, full, column, row_doc, col_doc = attention_specs(heads, length, rows)
    shape = jax.ShapeDtypeStruct((heads, length, HEAD), jnp.float32)
    return pl.pallas_call(
        backward_kernel,
        grid=(heads, length // rows),
        in_specs=[own, full, full, own, column, row_doc, col_doc],
        out_specs=[own, full, full],
        out_shape=[shape] * 3,
        compiler_params=pltpu.CompilerParams(vmem_limit_bytes=40 * 1024 * 1024),
        cost_estimate=pl.CostEstimate(
            flops=40 * heads * length * length * HEAD,
            bytes_accessed=20 * heads * length * HEAD,
            transcendentals=heads * length * length,
        ),
    )(queries, keys, values, grads, log_sums, docs[:, None], docs[None, :])


def on_device_packed(
    devices,
    ring,
    tokens,
    segments,
    cotangent,
    w_qkv,
    bias_q,
    bias_v,
    w_out,
    bias_out,
    gain_one,
    shift_one,
    w_up,
    bias_up,
    w_down,
    bias_down,
    gain_two,
    shift_two,
):
    both = ("dp", "seq")
    seq_count, slice_len, model_width = tokens.shape
    row_total = seq_count * slice_len
    own_rows = w_qkv.shape[0]
    fold = w_up.shape[1] // model_width
    down_rows = w_down.shape[0]
    vectors = (bias_q, bias_v, bias_out, gain_one, shift_one, bias_down, gain_two, shift_two)
    count = len(vectors)
    qkv_width = 3 * model_width

    rest = jnp.concatenate(
        [w_down, w_out] + [w_up[:, i * model_width : (i + 1) * model_width] for i in range(fold)],
        axis=0,
    )
    rest_all = lax.all_gather(rest, both, axis=0, tiled=False)
    groups = ring // seq_count
    width = model_width // groups
    heads = width // HEAD
    length = ring * slice_len
    extra = jnp.concatenate(
        [jnp.stack(vectors, axis=1), bias_up.reshape(own_rows, fold)], axis=1
    )
    extra = jnp.pad(extra, ((0, 0), (0, 128 - count - fold)))
    blocks = w_qkv.reshape(own_rows, 3, groups, width).transpose(2, 0, 1, 3)
    first = jnp.concatenate(
        [
            blocks.reshape(groups, own_rows, 3 * width),
            jnp.broadcast_to(extra[None], (groups,) + extra.shape),
        ],
        axis=2,
    )
    first = jnp.broadcast_to(
        first[None], (devices // groups,) + first.shape
    ).reshape(devices, own_rows, 3 * width + 128)
    first_all = lax.all_to_all(first, both, 0, 0, tiled=True).reshape(
        devices * own_rows, 3 * width + 128
    )
    w_qkv_own = first_all[:, : 3 * width]
    small = first_all[:, 3 * width : 3 * width + count + fold].astype(jnp.float32)
    bq, bv, bo, g1, s1, bd, g2, s2 = [small[:, i] for i in range(count)]
    bu = small[:, count:].reshape(-1)

    inputs = tokens.reshape(row_total, model_width)
    seq_inputs = lax.all_to_all(
        jnp.broadcast_to(
            tokens[:, None], (seq_count, groups, slice_len, model_width)
        ).reshape(ring, slice_len, model_width),
        "seq",
        0,
        0,
        tiled=True,
    ).reshape(length, model_width)
    place = lax.axis_index("seq")
    own_seq, own_group = place // groups, place % groups
    qkv_bias = jnp.concatenate(
        [
            lax.dynamic_slice_in_dim(bq, own_group * width, width, 0),
            jnp.zeros((width,), jnp.float32),
            lax.dynamic_slice_in_dim(bv, own_group * width, width, 0),
        ]
    )
    projected = (
        jnp.dot(seq_inputs, w_qkv_own, preferred_element_type=jnp.float32) + qkv_bias
    ).astype(jnp.bfloat16)
    own = projected.reshape(length, 3, heads, HEAD).transpose(1, 2, 0, 3)
    docs = lax.dynamic_index_in_dim(segments, own_seq, 0, keepdims=False)
    mixed_own, log_sums = local_forward(own[0], own[1], own[2], docs)
    mixed_sent = mixed_own.transpose(1, 0, 2).reshape(ring, slice_len, width)
    mixed = lax.all_to_all(mixed_sent, "seq", 0, 0, tiled=True)
    mixed_low = (
        mixed.reshape(seq_count, groups, slice_len, width)
        .transpose(0, 2, 1, 3)
        .reshape(row_total, model_width)
    )

    w_down_all = rest_all[:, :down_rows].reshape(-1, model_width)
    w_out_all = rest_all[:, down_rows : down_rows + own_rows].reshape(-1, model_width)
    up_start = down_rows + own_rows
    w_up_all = jnp.concatenate(
        [
            rest_all[:, up_start + i * own_rows : up_start + (i + 1) * own_rows].reshape(
                -1, model_width
            )
            for i in range(fold)
        ],
        axis=1,
    )
    branch = jnp.dot(mixed_low, w_out_all, preferred_element_type=jnp.float32) + bo
    normed_one, norm_one_back = jax.vjp(normalize, inputs.astype(jnp.float32) + branch, g1, s1)
    normed_low = normed_one.astype(jnp.bfloat16)
    hidden = jnp.dot(normed_low, w_up_all, preferred_element_type=jnp.float32) + bu
    activated, gelu_back = jax.vjp(exact_gelu, hidden)
    activated_low = activated.astype(jnp.bfloat16)
    feed = jnp.dot(activated_low, w_down_all, preferred_element_type=jnp.float32) + bd
    result, norm_two_back = jax.vjp(normalize, normed_one + feed, g2, s2)

    grad_sum_two, grad_gain_two, grad_shift_two = norm_two_back(
        cotangent.reshape(row_total, model_width).astype(jnp.float32)
    )
    grad_feed = grad_sum_two.astype(jnp.bfloat16)
    grad_w_down = contract_rows(activated_low, grad_feed).astype(jnp.bfloat16)
    grad_bias_down = column_sum(grad_feed)
    (grad_hidden,) = gelu_back(contract_cols(grad_feed, w_down_all))
    grad_hidden_low = grad_hidden.astype(jnp.bfloat16)
    grad_w_up = contract_rows(normed_low, grad_hidden_low).astype(jnp.bfloat16)
    grad_bias_up = column_sum(grad_hidden_low)
    grad_normed = grad_sum_two + contract_cols(grad_hidden_low, w_up_all)
    grad_sum_one, grad_gain_one, grad_shift_one = norm_one_back(grad_normed)
    grad_branch = grad_sum_one.astype(jnp.bfloat16)
    grad_w_out = contract_rows(mixed_low, grad_branch).astype(jnp.bfloat16)
    grad_bias_out = column_sum(grad_branch)

    packed = jnp.concatenate(
        [
            grad_w_down.reshape(devices, down_rows, model_width),
            grad_w_out.reshape(devices, own_rows, model_width),
        ]
        + [
            grad_w_up[:, i * model_width : (i + 1) * model_width].reshape(
                devices, own_rows, model_width
            )
            for i in range(fold)
        ],
        axis=1,
    )
    rest_sum = lax.psum_scatter(
        packed.reshape(-1, model_width), both, scatter_dimension=0, tiled=True
    ).astype(jnp.float32)

    grad_mixed = contract_cols(grad_branch, w_out_all).astype(jnp.bfloat16)
    grad_sent = (
        grad_mixed.reshape(seq_count, slice_len, groups, width)
        .transpose(0, 2, 1, 3)
        .reshape(ring, slice_len, width)
    )
    grad_own = lax.all_to_all(grad_sent, "seq", 0, 0, tiled=True)
    grad_own = grad_own.reshape(length, heads, HEAD).transpose(1, 0, 2)
    parts = local_backward(own[0], own[1], own[2], grad_own, log_sums, docs)
    grad_proj = (
        jnp.stack(parts).astype(jnp.bfloat16).transpose(2, 0, 1, 3).reshape(length, 3 * width)
    )
    token_part = contract_cols(grad_proj, w_qkv_own).astype(jnp.bfloat16)
    token_part = lax.all_to_all(
        token_part.reshape(ring, slice_len, model_width), "seq", 0, 0, tiled=True
    ).reshape(seq_count, groups, slice_len, model_width)
    grad_inputs = grad_sum_one.reshape(tokens.shape) + jnp.sum(
        token_part.astype(jnp.float32), axis=1
    )
    grad_w_qkv = contract_rows(seq_inputs, grad_proj)
    grad_qkv_bias = column_sum(grad_proj)

    def own_columns(values):
        spread = jnp.zeros((model_width,), jnp.float32)
        return lax.dynamic_update_slice_in_dim(spread, values, own_group * width, 0)

    grads = (
        own_columns(grad_qkv_bias[:width]),
        own_columns(grad_qkv_bias[2 * width :]),
        grad_bias_out,
        grad_gain_one,
        grad_shift_one,
        grad_bias_down,
        grad_gain_two,
        grad_shift_two,
    )
    extra = jnp.concatenate(
        [jnp.stack(grads, axis=1), grad_bias_up.reshape(-1, fold)], axis=1
    )
    last = jnp.concatenate(
        [grad_w_qkv, jnp.pad(extra, ((0, 0), (0, 128 - count - fold)))], axis=1
    ).astype(jnp.bfloat16)
    last = lax.all_to_all(
        last.reshape(devices, own_rows, 3 * width + 128), both, 0, 0, tiled=True
    ).astype(jnp.float32)
    last = jnp.sum(last.reshape(-1, groups, own_rows, 3 * width + 128), axis=0)
    own_qkv = (
        last[:, :, : 3 * width]
        .reshape(groups, own_rows, 3, width)
        .transpose(1, 2, 0, 3)
        .reshape(own_rows, qkv_width)
    )
    tail = jnp.sum(last[:, :, 3 * width :], axis=0)
    sums = [tail[:, i] for i in range(count)]
    own_up = jnp.concatenate(
        [rest_sum[up_start + i * own_rows : up_start + (i + 1) * own_rows] for i in range(fold)],
        axis=1,
    )
    return (
        result.astype(jnp.bfloat16).reshape(seq_count, slice_len, model_width),
        grad_inputs,
        own_qkv,
        sums[0],
        sums[1],
        rest_sum[down_rows : down_rows + own_rows],
        sums[2],
        sums[3],
        sums[4],
        own_up,
        tail[:, count : count + fold].reshape(-1),
        rest_sum[:down_rows],
        sums[5],
        sums[6],
        sums[7],
    )


def solution(mesh):
    ring = mesh.shape["seq"]
    devices = ring * mesh.shape["dp"]

    def on_device(*arguments):
        seq_count, _, model_width = arguments[0].shape
        heads = model_width // HEAD
        if ring % seq_count == 0 and heads % (ring // seq_count) == 0:
            return on_device_packed(devices, ring, *arguments)
        return on_device_general(*arguments)

    return jax.shard_map(
        on_device,
        mesh=mesh,
        in_specs=(
            P("dp", "seq", None),
            P("dp", None),
            P("dp", "seq", None),
            P(("dp", "seq"), None),
            P(("dp", "seq")),
            P(("dp", "seq")),
            P(("dp", "seq"), None),
            P(("dp", "seq")),
            P(("dp", "seq")),
            P(("dp", "seq")),
            P(("dp", "seq"), None),
            P(("dp", "seq")),
            P(("dp", "seq"), None),
            P(("dp", "seq")),
            P(("dp", "seq")),
            P(("dp", "seq")),
        ),
        out_specs=(
            P("dp", "seq", None),
            P("dp", "seq", None),
            P(("dp", "seq"), None),
            P(("dp", "seq")),
            P(("dp", "seq")),
            P(("dp", "seq"), None),
            P(("dp", "seq")),
            P(("dp", "seq")),
            P(("dp", "seq")),
            P(("dp", "seq"), None),
            P(("dp", "seq")),
            P(("dp", "seq"), None),
            P(("dp", "seq")),
            P(("dp", "seq")),
            P(("dp", "seq")),
        ),
        check_vma=False,
    )
```
